256 devices in a mesh: ctx: 16 (over x, y_hi, core), tp: 16 (over y_lo, z).
Axes of the slice: x: 4, y: 4 (y_hi: 2, y_lo: 2; y = y_hi * 2 + y_lo), z: 8, core: 2. Of those that a mesh axis runs over, the one named last changes fastest.
Arguments:
- queries: bfloat16 [8192, 8192], P('ctx', 'tp'), may hold values from -6 to 6
- keys: bfloat16 [8192, 8192], P('ctx', 'tp'), may hold values from -6 to 6
- values: bfloat16 [8192, 8192], P('ctx', 'tp'), may hold values from -6 to 6
- positions: int32 [8192], P('ctx'), may hold values from 0 to 2047, as said below
- lambda_query: float32 [32, 256], P('tp'), may hold values from -0.6 to 0.6
- lambda_key: float32 [32, 256], P('tp'), may hold values from -0.6 to 0.6
- norm_gain: float32 [256], replicated, may hold values from 0.25 to 1.75
- out_weight: bfloat16 [8192, 8192], P('tp'), may hold values from -0.0625 to 0.0625
Outputs:
- mixed: bfloat16 [8192, 8192], P(('ctx', 'tp'))
The draws below stay inside these ranges and needn't reach their ends.
Inputs may be any that keep to these rules, and one draw needn't show every extreme that they name: positions[j] counts token j's place in its document: 0 at a document's first token, rising by one per token. The batch holds 8 documents of 2 to 2048 tokens each, one of exactly 2048 tokens.
All inputs are finite; a program needn't handle non-finite values.
Results may differ from the reference program's by a relative error of at most 0.0059.
Values may be sent and summed in bfloat16 or wider, within the bound.
No kernel may reach another device: no remote copies, remote signals or barrier semaphores. Data moves between devices by JAX's collectives and lax.ppermute only.
A program may use at most 128 MiB of HBM per device.

```python
import math
import jax
import jax.numpy as jnp
from jax import lax

D = 8192
HEADS = 32
HD = 128
TOK_DEV = 512
DOCS = 8
TOKENS = 8192
MOST = 2048
REACH = 4


def doc_lengths(key):
    others = DOCS - 1
    remain = TOKENS - MOST
    middle = remain // others
    paired = others // 2
    jitter = jax.random.randint(jax.random.fold_in(key, 11), (paired,), -(middle // 2), middle // 2 + 1)
    lengths = jnp.full((others,), middle, jnp.int32)
    lengths = lengths.at[0:paired].add(jitter)
    lengths = lengths.at[paired:2 * paired].add(-jitter)
    lengths = lengths.at[others - 1].add(remain - others * middle)
    lengths = jnp.concatenate([jnp.full((1,), MOST, jnp.int32), lengths])
    order = jax.random.permutation(jax.random.fold_in(key, 12), DOCS)
    return lengths[order].astype(jnp.int32)


def document_bounds(key):
    lengths = doc_lengths(key)
    ends = jnp.cumsum(lengths).astype(jnp.int32)
    return ends - lengths


def draw_positions(key, part):
    starts = document_bounds(key)
    token_index = jnp.arange(TOKENS, dtype=jnp.int32)
    owner_start = jnp.max(jnp.where(token_index[:, None] >= starts[None, :], starts[None, :], 0), axis=1)
    return (token_index - owner_start).astype(jnp.int32)


def query_keys(key):
    columns = HEADS * 2 * HD
    query_all = jnp.clip(jax.random.normal(jax.random.fold_in(key, 33), (TOKENS, columns)), -5.0, 5.0)
    key_all = jnp.clip(jax.random.normal(jax.random.fold_in(key, 34), (TOKENS, columns)), -5.0, 5.0)
    return (query_all, key_all)


def draw_queries(key, part):
    return query_keys(key)[0].astype(jnp.bfloat16)


def draw_keys(key, part):
    return query_keys(key)[1].astype(jnp.bfloat16)


def block_scale(key, extent, cuts, smallest, largest):
    def one(position, parts):
        draws = jax.random.uniform(jax.random.fold_in(jax.random.fold_in(key, 6), position), (parts,), jnp.float32, smallest / len(cuts), largest / len(cuts))
        return jnp.repeat(jnp.exp(draws), extent[position] // parts).reshape((-1,) + (1,) * (len(extent) - position - 1))

    gain = one(*cuts[0])
    for cut in cuts[1:]:
        gain = gain * one(*cut)
    return gain


def bell_draw(rng, dims, width, limit, pieces=(), kind=jnp.bfloat16):
    loudness = block_scale(rng, dims, pieces, -0.22, 0.18) if pieces else 1.0
    array = jax.random.normal(rng, dims, jnp.float32) * width * loudness
    return jnp.minimum(jnp.maximum(array, -limit), limit).astype(kind)


def setup_inputs(seed: int = 0) -> dict:
    seeds = jax.random.split(jax.random.key(seed), 9)
    return {
        "queries": draw_queries(jax.random.fold_in(seeds[8], 71), 0),
        "keys": draw_keys(jax.random.fold_in(seeds[8], 71), 0),
        "values": bell_draw(seeds[2], (TOKENS, HEADS * 2 * HD), 1.0, 6.0, ((0, 16), (1, 16))),
        "positions": draw_positions(jax.random.fold_in(seeds[8], 71), 0),
        "lambda_query": bell_draw(seeds[4], (HEADS, 2 * HD), 0.15, 0.6, ((0, 16),), jnp.float32),
        "lambda_key": bell_draw(seeds[5], (HEADS, 2 * HD), 0.15, 0.6, ((0, 16),), jnp.float32),
        "norm_gain": jnp.clip(1.0 + 0.15 * jax.random.normal(seeds[6], (2 * HD,), jnp.float32), 0.25, 1.75),
        "out_weight": bell_draw(seeds[7], (HEADS * 2 * HD, D), (HEADS * 2 * HD) ** -0.5, 0.0625, ((0, 16),)),
    }


NEG = -1e+30
EPS = 1e-05
LAMBDA_INIT = 0.8 - 0.6 * math.exp(-3.3)

def reference(queries, keys, values, positions, lambda_query, lambda_key, norm_gain, out_weight):
    total = queries.shape[0]
    head_width = 2 * HD
    window = REACH * TOK_DEV
    token_index = jnp.arange(total, dtype=jnp.int32)
    doc_start = token_index - positions
    lambda_head = jnp.exp(lax.optimization_barrier(jnp.sum(lambda_query[:, :HD] * lambda_key[:, :HD], axis=1))) - jnp.exp(lax.optimization_barrier(jnp.sum(lambda_query[:, HD:] * lambda_key[:, HD:], axis=1))) + LAMBDA_INIT
    padded_keys = jnp.concatenate([jnp.zeros((window, keys.shape[1]), keys.dtype), keys], 0)
    padded_values = jnp.concatenate([jnp.zeros((window, values.shape[1]), values.dtype), values], 0)
    block_count = total // TOK_DEV

    def one_head(head_idx):
        column = (head_idx * head_width).astype(jnp.int32)
        head_q = lax.dynamic_slice_in_dim(queries, column, head_width, 1).reshape(total, 2, HD)
        head_k = lax.dynamic_slice_in_dim(padded_keys, column, head_width, 1).reshape(total + window, 2, HD)
        head_v = lax.dynamic_slice_in_dim(padded_values, column, head_width, 1)

        def one_block(block_idx):
            first = (block_idx * TOK_DEV).astype(jnp.int32)
            block_q = lax.dynamic_slice_in_dim(head_q, first, TOK_DEV, 0)
            block_k = lax.dynamic_slice_in_dim(head_k, first, TOK_DEV + window, 0)
            block_v = lax.dynamic_slice_in_dim(head_v, first, TOK_DEV + window, 0)
            query_pos = first + jnp.arange(TOK_DEV, dtype=jnp.int32)
            key_pos = first - window + jnp.arange(TOK_DEV + window, dtype=jnp.int32)
            starts = lax.dynamic_slice_in_dim(doc_start, first, TOK_DEV, 0)
            live = (key_pos[None, :] >= starts[:, None]) & (key_pos[None, :] <= query_pos[:, None])
            scores = jnp.einsum('qmd,kmd->mqk', block_q.astype(jnp.float32), block_k.astype(jnp.float32)) * HD ** (-0.5)
            scores = jnp.where(live[None], scores, NEG)
            row_max = lax.optimization_barrier(jnp.max(scores, axis=-1, keepdims=True))
            weights = jnp.where(live[None], jnp.exp(scores - row_max), 0.0)
            totals = lax.optimization_barrier(jnp.sum(weights, axis=-1))
            rounded = lax.optimization_barrier(weights.astype(jnp.bfloat16)).astype(jnp.float32)
            summed = jnp.einsum('mqk,ke->mqe', rounded, block_v.astype(jnp.float32))
            combined = summed[0] / totals[0][:, None] - lambda_head[head_idx] * summed[1] / totals[1][:, None]
            normed = combined * lax.rsqrt(lax.optimization_barrier(jnp.mean(combined * combined, axis=-1, keepdims=True)) + EPS)
            return (normed * norm_gain * (1.0 - LAMBDA_INIT)).astype(jnp.bfloat16)
        return lax.map(one_block, jnp.arange(block_count, dtype=jnp.int32))
    head_out = lax.map(one_head, jnp.arange(HEADS, dtype=jnp.int32))
    attended = jnp.transpose(head_out, (1, 2, 0, 3)).reshape(total, HEADS * head_width)
    return jnp.dot(attended, out_weight, preferred_element_type=jnp.float32).astype(jnp.bfloat16)
```

```python
import functools
import math

import jax
import jax.numpy as jnp
from jax import lax
from jax.experimental import pallas as pl
from jax.experimental.pallas import tpu as pltpu
from jax.sharding import PartitionSpec as P

EPS = 1e-05
LAMBDA_INIT = 0.8 - 0.6 * math.exp(-3.3)
NEG = -1e30
HD = 128
TOK = 512
TILE = 256
GROUP = 4
MIB = 1024 * 1024


def segments(tile):
    first = tile * TILE
    parts = [(0, 0, first + TILE)]
    parts += [(offset, 0, TOK) for offset in (1, 2, 3)]
    parts.append((4, first, TOK))
    return parts


def attention_kernel(start_ref, lambda_ref, gain_ref, q_ref, *refs):
    blocks, out_ref, score_ref = refs[:5], refs[5], refs[6]
    factor = HD**-0.5 * math.log2(math.e)
    for tile in range(TOK // TILE):
        rows = pl.ds(tile * TILE, TILE)
        starts = start_ref[rows, :]
        ratio = []
        for which in range(2):
            columns = slice(which * HD, (which + 1) * HD)
            query = q_ref[rows, columns]
            best = jnp.full((TILE, HD), NEG, jnp.float32)
            at = 0
            places = []
            for offset, low, high in segments(tile):
                size = high - low
                score = (
                    lax.dot_general(
                        query,
                        blocks[offset][low:high, columns],
                        (((1,), (1,)), ((), ())),
                        preferred_element_type=jnp.float32,
                    )
                    * factor
                )
                key = lax.broadcasted_iota(jnp.int32, (TILE, size), 1) + (low - offset * TOK)
                live = key >= starts
                if offset == 0:
                    token = lax.broadcasted_iota(jnp.int32, (TILE, size), 0) + tile * TILE
                    live = live & (key <= token)
                score = jnp.where(live, score, NEG)
                score_ref[:, at : at + size] = score
                for piece in range(0, size, HD):
                    best = jnp.maximum(best, score[:, piece : piece + HD])
                places.append((offset, low, high, at))
                at += size
            row_max = jnp.max(best, axis=1, keepdims=True)
            total = jnp.zeros((TILE, HD), jnp.float32)
            summed = jnp.zeros((TILE, 2 * HD), jnp.float32)
            for offset, low, high, at in places:
                size = high - low
                weight = jnp.exp2(score_ref[:, at : at + size] - row_max)
                for piece in range(0, size, HD):
                    total = total + weight[:, piece : piece + HD]
                summed = summed + jnp.dot(
                    weight.astype(jnp.bfloat16),
                    blocks[offset][low:high, 2 * HD :],
                    preferred_element_type=jnp.float32,
                )
            ratio.append(summed / jnp.sum(total, axis=1, keepdims=True))
        combined = ratio[0] - lambda_ref[0] * ratio[1]
        power = jnp.mean(combined * combined, axis=1, keepdims=True)
        out_ref[rows, :] = (
            combined * lax.rsqrt(power + EPS) * gain_ref[...] * (1.0 - LAMBDA_INIT)
        ).astype(jnp.bfloat16)


def attention(starts, scale, gain, query, blocks):
    vmem = pl.BlockSpec(memory_space=pltpu.VMEM)
    return pl.pallas_call(
        attention_kernel,
        out_shape=jax.ShapeDtypeStruct((TOK, 2 * HD), jnp.bfloat16),
        in_specs=[vmem, pl.BlockSpec(memory_space=pltpu.SMEM)] + [vmem] * 7,
        out_specs=vmem,
        scratch_shapes=[pltpu.VMEM((TILE, 5 * TOK), jnp.float32)],
        compiler_params=pltpu.CompilerParams(vmem_limit_bytes=24 * MIB),
        cost_estimate=pl.CostEstimate(
            flops=2 * 2 * TOK * 5 * TOK * 3 * HD, bytes_accessed=3 * MIB, transcendentals=2 * TOK * 5 * TOK
        ),
    )(starts, scale, gain, query, *blocks)


def project_kernel(*refs):
    attended, weights, out_ref = refs[:8], refs[8:16], refs[16]
    half = weights[0].shape[1]
    step = 256
    for side in range(2):
        for column in range(0, half, step):
            total = None
            for member in range(4):
                for head in range(2):
                    term = jnp.dot(
                        attended[member * 2 + head][...],
                        weights[side * 4 + member][head * 256 : (head + 1) * 256, column : column + step],
                        preferred_element_type=jnp.float32,
                    )
                    total = term if total is None else total + term
            out_ref[:, side * half + column : side * half + column + step] = total.astype(jnp.bfloat16)


def project(attended, weights):
    vmem = pl.BlockSpec(memory_space=pltpu.VMEM)
    half = weights[0].shape[1]
    return pl.pallas_call(
        project_kernel,
        out_shape=jax.ShapeDtypeStruct((TOK, 2 * half), jnp.bfloat16),
        in_specs=[vmem] * 16,
        out_specs=vmem,
        compiler_params=pltpu.CompilerParams(vmem_limit_bytes=32 * MIB),
        cost_estimate=pl.CostEstimate(
            flops=2 * TOK * 2048 * 2 * half, bytes_accessed=12 * MIB, transcendentals=0
        ),
    )(*attended, *weights)


def total_kernel(core_ref, parts_ref, out_ref):
    half = parts_ref.shape[2] // 2
    for member in range(4):
        high, low = divmod(member, 2)
        for side in range(2):
            total = None
            for pair in range(4):
                source = high * 8 + pair * 2 + low
                term = parts_ref[source, :, side * half : (side + 1) * half].astype(jnp.float32)
                total = term if total is None else total + term
            place = member * 2 * half + (core_ref[0] if side == 0 else 1 - core_ref[0]) * half
            out_ref[:, pl.ds(pl.multiple_of(place, half), half)] = total.astype(jnp.bfloat16)


def total_up(core, parts):
    vmem = pl.BlockSpec(memory_space=pltpu.VMEM)
    return pl.pallas_call(
        total_kernel,
        out_shape=jax.ShapeDtypeStruct((parts.shape[1], 4 * parts.shape[2]), jnp.bfloat16),
        in_specs=[pl.BlockSpec(memory_space=pltpu.SMEM), vmem],
        out_specs=vmem,
        compiler_params=pltpu.CompilerParams(vmem_limit_bytes=16 * MIB),
    )(core, parts)


def later(value, steps):
    count = lax.axis_size("ctx")
    return lax.ppermute(value, "ctx", [(i, i + steps) for i in range(count - steps)])


def across(value):
    return lax.ppermute(value, "ctx", [(i, i ^ 1) for i in range(lax.axis_size("ctx"))])


def partner(value, member):
    high, low = divmod(member, 2)
    pairs = [(t, (((t // 8) ^ high) * 8) + ((t % 8) ^ low)) for t in range(lax.axis_size("tp"))]
    return lax.ppermute(value, "tp", pairs)


def shards(queries, keys, values, positions, lambda_query, lambda_key, norm_gain, out_weight):
    ctx = lax.axis_index("ctx")
    tp = lax.axis_index("tp")
    core = lax.rem(ctx, 2)
    own = (tp // 8) * 2 + lax.rem(tp, 2)
    starts = (jnp.arange(TOK, dtype=jnp.int32) - positions)[:, None]
    lambda_head = (
        jnp.exp(jnp.sum(lambda_query[:, :HD] * lambda_key[:, :HD], axis=1))
        - jnp.exp(jnp.sum(lambda_query[:, HD:] * lambda_key[:, HD:], axis=1))
        + LAMBDA_INIT
    )
    gain = norm_gain[None, :]
    width = 2 * HD

    pairs = []
    for head in range(2):
        part = slice(head * width, (head + 1) * width)
        here = jnp.concatenate([keys[:, part], values[:, part]], axis=1)
        pairs.append((here, later(here, 2), later(here, 4)))

    side = out_weight.shape[1] // GROUP // 2

    def weight_part(member, half):
        place = (own ^ member) * (2 * side) + half * side
        return lax.dynamic_slice(out_weight, (0, place), (out_weight.shape[0], side))

    mine = [weight_part(0, core)] + [partner(weight_part(d, core), d) for d in (1, 2, 3)]
    other = [weight_part(0, 1 - core)] + [across(piece) for piece in mine[1:]]

    attended = []
    for head in range(2):
        here, two, four = pairs[head]
        even = core == 0
        one, three = across((jnp.where(even, here, two), jnp.where(even, two, four)))
        result = attention(
            starts,
            lambda_head[head : head + 1],
            gain,
            queries[:, head * width : (head + 1) * width],
            [here, one, two, three, four],
        )
        attended.append([result] + [partner(result, d) for d in (1, 2, 3)])
    flat = [attended[head][member] for member in range(4) for head in range(2)]
    partial = project(flat, mine + other)
    count = lax.axis_size("tp")
    parts = lax.all_to_all(partial.reshape(count, TOK // count, 2 * side), "tp", 0, 0)
    return total_up(core[None], parts)


def solution(mesh):
    return jax.shard_map(
        shards,
        mesh=mesh,
        in_specs=(
            P("ctx", "tp"),
            P("ctx", "tp"),
            P("ctx", "tp"),
            P("ctx"),
            P("tp", None),
            P("tp", None),
            P(),
            P("tp", None),
        ),
        out_specs=P(("ctx", "tp"), None),
        check_vma=False,
    )
```

```python
import functools
import math

import jax
import jax.numpy as jnp
from jax import lax
from jax.experimental import pallas as pl
from jax.experimental.pallas import tpu as pltpu
from jax.sharding import PartitionSpec as P

EPS = 1e-05
LAMBDA_INIT = 0.8 - 0.6 * math.exp(-3.3)
NEG = -1e30
HD = 128
TOK = 512
TILE = 256
GROUP = 4
MIB = 1024 * 1024


def segments(tile):
    first = tile * TILE
    parts = [(0, 0, first + TILE)]
    parts += [(offset, 0, TOK) for offset in (1, 2, 3)]
    parts.append((4, first, TOK))
    return parts


def pack_kernel(keys_ref, values_ref, out_ref, sems):
    width = keys_ref.shape[1]
    copies = [
        pltpu.make_async_copy(keys_ref, out_ref.at[:, pl.ds(0, width)], sems.at[0]),
        pltpu.make_async_copy(values_ref, out_ref.at[:, pl.ds(width, width)], sems.at[1]),
    ]
    for copy in copies:
        copy.start()
    for copy in copies:
        copy.wait()


def pack(keys, values):
    whole = pl.BlockSpec(memory_space=pl.ANY)
    return pl.pallas_call(
        pack_kernel,
        out_shape=jax.ShapeDtypeStruct((TOK, 8 * HD), jnp.bfloat16),
        in_specs=[whole] * 2,
        out_specs=whole,
        scratch_shapes=[pltpu.SemaphoreType.DMA((2,))],
        cost_estimate=pl.CostEstimate(flops=0, bytes_accessed=2 * MIB, transcendentals=0),
    )(keys, values)


def attention_kernel(
    head, core_ref, start_ref, lambda_ref, gain_ref, q_ref, keys_ref, values_ref,
    twin_ref, two_ref, other_ref, four_ref, out_ref, score_ref,
):
    width = 2 * HD
    key_column, value_column = head * width, (2 + head) * width
    back = [0, 1 + 2 * core_ref[0], 2, 3 - 2 * core_ref[0], 4]
    key_refs = [keys_ref, twin_ref, two_ref, other_ref, four_ref]
    value_refs = [values_ref] + key_refs[1:]
    factor = HD**-0.5 * math.log2(math.e)
    for tile in range(TOK // TILE):
        rows = pl.ds(tile * TILE, TILE)
        starts = start_ref[rows, :]
        ratio = []
        for which in range(2):
            column = head * width + which * HD
            query = q_ref[rows, column : column + HD]
            best = jnp.full((TILE, HD), NEG, jnp.float32)
            at = 0
            places = []
            for offset, low, high in segments(tile):
                size = high - low
                column = key_column + which * HD
                score = (
                    lax.dot_general(
                        query,
                        key_refs[offset][low:high, column : column + HD],
                        (((1,), (1,)), ((), ())),
                        preferred_element_type=jnp.float32,
                    )
                    * factor
                )
                key = lax.broadcasted_iota(jnp.int32, (TILE, size), 1) + (low - back[offset] * TOK)
                live = key >= starts
                if offset == 0:
                    token = lax.broadcasted_iota(jnp.int32, (TILE, size), 0) + tile * TILE
                    live = live & (key <= token)
                score = jnp.where(live, score, NEG)
                score_ref[:, at : at + size] = score
                for piece in range(0, size, HD):
                    best = jnp.maximum(best, score[:, piece : piece + HD])
                places.append((offset, low, high, at))
                at += size
            row_max = jnp.max(best, axis=1, keepdims=True)
            total = jnp.zeros((TILE, HD), jnp.float32)
            summed = jnp.zeros((TILE, width), jnp.float32)
            for offset, low, high, at in places:
                size = high - low
                column = key_column if offset == 0 else value_column
                weight = jnp.exp2(score_ref[:, at : at + size] - row_max)
                for piece in range(0, size, HD):
                    total = total + weight[:, piece : piece + HD]
                summed = summed + jnp.dot(
                    weight.astype(jnp.bfloat16),
                    value_refs[offset][low:high, column : column + width],
                    preferred_element_type=jnp.float32,
                )
            ratio.append(summed / jnp.sum(total, axis=1, keepdims=True))
        combined = ratio[0] - lambda_ref[head] * ratio[1]
        power = jnp.mean(combined * combined, axis=1, keepdims=True)
        out_ref[rows, :] = (
            combined * lax.rsqrt(power + EPS) * gain_ref[...] * (1.0 - LAMBDA_INIT)
        ).astype(jnp.bfloat16)


def attention(head, core, starts, scale, gain, query, keys, values, blocks):
    vmem = pl.BlockSpec(memory_space=pltpu.VMEM)
    smem = pl.BlockSpec(memory_space=pltpu.SMEM)
    return pl.pallas_call(
        functools.partial(attention_kernel, head),
        out_shape=jax.ShapeDtypeStruct((TOK, 2 * HD), jnp.bfloat16),
        in_specs=[smem, vmem, smem] + [vmem] * 8,
        out_specs=vmem,
        scratch_shapes=[pltpu.VMEM((TILE, 5 * TOK), jnp.float32)],
        compiler_params=pltpu.CompilerParams(vmem_limit_bytes=24 * MIB),
        cost_estimate=pl.CostEstimate(
            flops=2 * 2 * TOK * 5 * TOK * 3 * HD, bytes_accessed=3 * MIB, transcendentals=2 * TOK * 5 * TOK
        ),
    )(core, starts, scale, gain, query, keys, values, *blocks)


def project_kernel(*refs):
    attended, weights, out_ref = refs[:8], (refs[8:10], refs[10:12]), refs[12]
    half = weights[0][0].shape[1]
    step = 256
    for side in range(2):
        near, far = weights[side]
        for column in range(0, half, step):
            total = None
            for head in range(2):
                for member in range(4):
                    first = head * 256
                    if member == 0:
                        weight = near[first : first + 256, column : column + step]
                    else:
                        first += (member - 1) * TOK
                        weight = far[first : first + 256, column : column + step]
                    term = jnp.dot(
                        attended[head * 4 + member][...], weight, preferred_element_type=jnp.float32
                    )
                    total = term if total is None else total + term
            at = side * half + column
            out_ref[:, at : at + step] = total.astype(jnp.bfloat16)


def project(attended, weights):
    vmem = pl.BlockSpec(memory_space=pltpu.VMEM)
    wide = 2 * weights[0].shape[1]
    return pl.pallas_call(
        project_kernel,
        out_shape=jax.ShapeDtypeStruct((TOK, wide), jnp.bfloat16),
        in_specs=[vmem] * 12,
        out_specs=vmem,
        compiler_params=pltpu.CompilerParams(vmem_limit_bytes=32 * MIB),
        cost_estimate=pl.CostEstimate(
            flops=2 * TOK * 2048 * wide, bytes_accessed=12 * MIB, transcendentals=0
        ),
    )(*attended, *weights)


def total_kernel(core_ref, parts_ref, out_ref):
    half = parts_ref.shape[2] // 2
    for member in range(4):
        high, low = divmod(member, 2)
        for side in range(2):
            total = None
            for pair in range(4):
                source = high * 8 + pair * 2 + low
                term = parts_ref[source, :, side * half : (side + 1) * half].astype(jnp.float32)
                total = term if total is None else total + term
            place = member * 2 * half + (core_ref[0] if side == 0 else 1 - core_ref[0]) * half
            out_ref[:, pl.ds(pl.multiple_of(place, half), half)] = total.astype(jnp.bfloat16)


def total_up(core, parts):
    vmem = pl.BlockSpec(memory_space=pltpu.VMEM)
    return pl.pallas_call(
        total_kernel,
        out_shape=jax.ShapeDtypeStruct((parts.shape[1], 4 * parts.shape[2]), jnp.bfloat16),
        in_specs=[pl.BlockSpec(memory_space=pltpu.SMEM), vmem],
        out_specs=vmem,
        compiler_params=pltpu.CompilerParams(vmem_limit_bytes=16 * MIB),
    )(core, parts)


def later(value, steps):
    count = lax.axis_size("ctx")
    return lax.ppermute(value, "ctx", [(i, i + steps) for i in range(count - steps)])


def across(value):
    return lax.ppermute(value, "ctx", [(i, i ^ 1) for i in range(lax.axis_size("ctx"))])


def partner(value, member):
    high, low = divmod(member, 2)
    pairs = [(t, (((t // 8) ^ high) * 8) + ((t % 8) ^ low)) for t in range(lax.axis_size("tp"))]
    return lax.ppermute(value, "tp", pairs)


def weight_partner(value, member):
    high, low = divmod(member, 2)
    count = lax.axis_size("tp")
    pairs = []
    for c in range(lax.axis_size("ctx")):
        there = c ^ 2 if high and c % 2 else c
        for t in range(count):
            pairs.append((c * count + t, there * count + (((t // 8) ^ high) * 8) + ((t % 8) ^ low)))
    return lax.ppermute(value, ("ctx", "tp"), pairs)


def after(values, *results):
    return lax.optimization_barrier((values, results))[0]


def shards(queries, keys, values, positions, lambda_query, lambda_key, norm_gain, out_weight):
    ctx = lax.axis_index("ctx")
    tp = lax.axis_index("tp")
    core = lax.rem(ctx, 2)
    own = (tp // 8) * 2 + lax.rem(tp, 2)
    starts = (jnp.arange(TOK, dtype=jnp.int32) - positions)[:, None]
    lambda_head = (
        jnp.exp(jnp.sum(lambda_query[:, :HD] * lambda_key[:, :HD], axis=1))
        - jnp.exp(jnp.sum(lambda_query[:, HD:] * lambda_key[:, HD:], axis=1))
        + LAMBDA_INIT
    )
    gain = norm_gain[None, :]
    width = 2 * HD

    here = pack(keys, values)
    side = out_weight.shape[1] // GROUP // 2

    def weight_part(member, half):
        place = (own ^ member) * (2 * side) + half * side
        return lax.dynamic_slice(out_weight, (0, place), (out_weight.shape[0], side))

    def attend(head, blocks):
        return attention(head, core[None], starts, lambda_head, gain, queries, keys, values, blocks)

    slices = [weight_part(d, core) for d in (1, 2, 3)]
    two = later(here, 2)
    four = later(after(here, *slices), 4)
    mine = [weight_partner(part, d) for part, d in zip(slices, (1, 2, 3))]
    other = across(jnp.where(core == 0, here, four))
    blocks = [across(two), two, other, four]
    first = attend(0, blocks)
    gathered = [partner(first, d) for d in (1, 2, 3)]
    second = attend(1, blocks)
    far = jnp.concatenate(mine, axis=0)
    swapped = across(after(far, first))
    second, gathered[0] = after((second, gathered[0]), second)
    both = [first, *gathered, second] + [partner(second, d) for d in (1, 2, 3)]
    partial = project(both, [weight_part(0, core), far, weight_part(0, 1 - core), swapped])
    count = lax.axis_size("tp")
    parts = lax.all_to_all(partial.reshape(count, TOK // count, 2 * side), "tp", 0, 0)
    return total_up(core[None], parts)


def solution(mesh):
    return jax.shard_map(
        shards,
        mesh=mesh,
        in_specs=(
            P("ctx", "tp"),
            P("ctx", "tp"),
            P("ctx", "tp"),
            P("ctx"),
            P("tp", None),
            P("tp", None),
            P(),
            P("tp", None),
        ),
        out_specs=P(("ctx", "tp"), None),
        check_vma=False,
    )
```

```python
import functools
import math

import jax
import jax.numpy as jnp
from jax import lax
from jax.experimental import pallas as pl
from jax.experimental.pallas import tpu as pltpu
from jax.sharding import PartitionSpec as P

EPS = 1e-05
LAMBDA_INIT = 0.8 - 0.6 * math.exp(-3.3)
NEG = -1e30
HD = 128
TOK = 512
TILE = 256
GROUP = 4
MIB = 1024 * 1024


def segments(tile):
    first = tile * TILE
    parts = [(0, 0, first + TILE)]
    parts += [(offset, 0, TOK) for offset in (1, 2, 3)]
    parts.append((4, first, TOK))
    return parts


def pack_kernel(keys_ref, values_ref, out_ref, sems):
    width = keys_ref.shape[1]
    copies = [
        pltpu.make_async_copy(keys_ref, out_ref.at[:, pl.ds(0, width)], sems.at[0]),
        pltpu.make_async_copy(values_ref, out_ref.at[:, pl.ds(width, width)], sems.at[1]),
    ]
    for copy in copies:
        copy.start()
    for copy in copies:
        copy.wait()


def pack(keys, values):
    whole = pl.BlockSpec(memory_space=pl.ANY)
    return pl.pallas_call(
        pack_kernel,
        out_shape=jax.ShapeDtypeStruct((TOK, 8 * HD), jnp.bfloat16),
        in_specs=[whole] * 2,
        out_specs=whole,
        scratch_shapes=[pltpu.SemaphoreType.DMA((2,))],
        cost_estimate=pl.CostEstimate(flops=0, bytes_accessed=2 * MIB, transcendentals=0),
    )(keys, values)


def attention_kernel(
    head, core_ref, start_ref, lambda_ref, gain_ref, q_ref, keys_ref, values_ref,
    twin_ref, two_ref, other_ref, four_ref, out_ref, score_ref,
):
    width = 2 * HD
    key_column, value_column = head * width, (2 + head) * width
    back = [0, 1 + 2 * core_ref[0], 2, 3 - 2 * core_ref[0], 4]
    key_refs = [keys_ref, twin_ref, two_ref, other_ref, four_ref]
    value_refs = [values_ref] + key_refs[1:]
    factor = HD**-0.5 * math.log2(math.e)
    for tile in range(TOK // TILE):
        rows = pl.ds(tile * TILE, TILE)
        starts = start_ref[rows, :]
        ratio = []
        for which in range(2):
            column = head * width + which * HD
            query = q_ref[rows, column : column + HD]
            best = jnp.full((TILE, HD), NEG, jnp.float32)
            at = 0
            places = []
            for offset, low, high in segments(tile):
                size = high - low
                column = key_column + which * HD
                score = (
                    lax.dot_general(
                        query,
                        key_refs[offset][low:high, column : column + HD],
                        (((1,), (1,)), ((), ())),
                        preferred_element_type=jnp.float32,
                    )
                    * factor
                )
                key = lax.broadcasted_iota(jnp.int32, (TILE, size), 1) + (low - back[offset] * TOK)
                live = key >= starts
                if offset == 0:
                    token = lax.broadcasted_iota(jnp.int32, (TILE, size), 0) + tile * TILE
                    live = live & (key <= token)
                score = jnp.where(live, score, NEG)
                score_ref[:, at : at + size] = score
                for piece in range(0, size, HD):
                    best = jnp.maximum(best, score[:, piece : piece + HD])
                places.append((offset, low, high, at))
                at += size
            row_max = jnp.max(best, axis=1, keepdims=True)
            total = jnp.zeros((TILE, HD), jnp.float32)
            summed = jnp.zeros((TILE, width), jnp.float32)
            for offset, low, high, at in places:
                size = high - low
                column = key_column if offset == 0 else value_column
                weight = jnp.exp2(score_ref[:, at : at + size] - row_max)
                for piece in range(0, size, HD):
                    total = total + weight[:, piece : piece + HD]
                summed = summed + jnp.dot(
                    weight.astype(jnp.bfloat16),
                    value_refs[offset][low:high, column : column + width],
                    preferred_element_type=jnp.float32,
                )
            ratio.append(summed / jnp.sum(total, axis=1, keepdims=True))
        combined = ratio[0] - lambda_ref[head] * ratio[1]
        power = jnp.mean(combined * combined, axis=1, keepdims=True)
        out_ref[rows, :] = (
            combined * lax.rsqrt(power + EPS) * gain_ref[...] * (1.0 - LAMBDA_INIT)
        ).astype(jnp.bfloat16)


def attention(head, core, starts, scale, gain, query, keys, values, blocks):
    vmem = pl.BlockSpec(memory_space=pltpu.VMEM)
    smem = pl.BlockSpec(memory_space=pltpu.SMEM)
    return pl.pallas_call(
        functools.partial(attention_kernel, head),
        out_shape=jax.ShapeDtypeStruct((TOK, 2 * HD), jnp.bfloat16),
        in_specs=[smem, vmem, smem] + [vmem] * 8,
        out_specs=vmem,
        scratch_shapes=[pltpu.VMEM((TILE, 5 * TOK), jnp.float32)],
        compiler_params=pltpu.CompilerParams(vmem_limit_bytes=24 * MIB),
        cost_estimate=pl.CostEstimate(
            flops=2 * 2 * TOK * 5 * TOK * 3 * HD, bytes_accessed=3 * MIB, transcendentals=2 * TOK * 5 * TOK
        ),
    )(core, starts, scale, gain, query, keys, values, *blocks)


def project_kernel(*refs):
    attended, weights, out_ref = refs[:8], (refs[8:10], refs[10:12]), refs[12]
    half = weights[0][0].shape[1]
    step = 256
    for side in range(2):
        near, far = weights[side]
        for column in range(0, half, step):
            total = None
            for head in range(2):
                for member in range(4):
                    first = head * 256
                    if member == 0:
                        weight = near[first : first + 256, column : column + step]
                    else:
                        first += (member - 1) * TOK
                        weight = far[first : first + 256, column : column + step]
                    term = jnp.dot(
                        attended[head * 4 + member][...], weight, preferred_element_type=jnp.float32
                    )
                    total = term if total is None else total + term
            at = side * half + column
            out_ref[:, at : at + step] = total.astype(jnp.bfloat16)


def project(attended, weights):
    vmem = pl.BlockSpec(memory_space=pltpu.VMEM)
    wide = 2 * weights[0].shape[1]
    return pl.pallas_call(
        project_kernel,
        out_shape=jax.ShapeDtypeStruct((TOK, wide), jnp.bfloat16),
        in_specs=[vmem] * 12,
        out_specs=vmem,
        compiler_params=pltpu.CompilerParams(vmem_limit_bytes=32 * MIB),
        cost_estimate=pl.CostEstimate(
            flops=2 * TOK * 2048 * wide, bytes_accessed=12 * MIB, transcendentals=0
        ),
    )(*attended, *weights)


def total_kernel(core_ref, parts_ref, out_ref):
    half = parts_ref.shape[2] // 2
    for member in range(4):
        high, low = divmod(member, 2)
        for side in range(2):
            total = None
            for pair in range(4):
                source = high * 8 + pair * 2 + low
                term = parts_ref[source, :, side * half : (side + 1) * half].astype(jnp.float32)
                total = term if total is None else total + term
            place = member * 2 * half + (core_ref[0] if side == 0 else 1 - core_ref[0]) * half
            out_ref[:, pl.ds(pl.multiple_of(place, half), half)] = total.astype(jnp.bfloat16)


def total_up(core, parts):
    vmem = pl.BlockSpec(memory_space=pltpu.VMEM)
    return pl.pallas_call(
        total_kernel,
        out_shape=jax.ShapeDtypeStruct((parts.shape[1], 4 * parts.shape[2]), jnp.bfloat16),
        in_specs=[pl.BlockSpec(memory_space=pltpu.SMEM), vmem],
        out_specs=vmem,
        compiler_params=pltpu.CompilerParams(vmem_limit_bytes=16 * MIB),
    )(core, parts)


def later(value, steps):
    count = lax.axis_size("ctx")
    return lax.ppermute(value, "ctx", [(i, i + steps) for i in range(count - steps)])


def across(value):
    return lax.ppermute(value, "ctx", [(i, i ^ 1) for i in range(lax.axis_size("ctx"))])


def partner(value, member):
    high, low = divmod(member, 2)
    pairs = [(t, (((t // 8) ^ high) * 8) + ((t % 8) ^ low)) for t in range(lax.axis_size("tp"))]
    return lax.ppermute(value, "tp", pairs)


def weight_partner(value, member):
    high, low = divmod(member, 2)
    count = lax.axis_size("tp")
    pairs = []
    for c in range(lax.axis_size("ctx")):
        there = c ^ 2 if high and c % 2 else c
        for t in range(count):
            pairs.append((c * count + t, there * count + (((t // 8) ^ high) * 8) + ((t % 8) ^ low)))
    return lax.ppermute(value, ("ctx", "tp"), pairs)


def after(values, *results):
    return lax.optimization_barrier((values, results))[0]


def shards(queries, keys, values, positions, lambda_query, lambda_key, norm_gain, out_weight):
    ctx = lax.axis_index("ctx")
    tp = lax.axis_index("tp")
    core = lax.rem(ctx, 2)
    own = (tp // 8) * 2 + lax.rem(tp, 2)
    starts = (jnp.arange(TOK, dtype=jnp.int32) - positions)[:, None]
    lambda_head = (
        jnp.exp(jnp.sum(lambda_query[:, :HD] * lambda_key[:, :HD], axis=1))
        - jnp.exp(jnp.sum(lambda_query[:, HD:] * lambda_key[:, HD:], axis=1))
        + LAMBDA_INIT
    )
    gain = norm_gain[None, :]
    width = 2 * HD

    here = jnp.concatenate([keys, values], axis=1)
    side = out_weight.shape[1] // GROUP // 2

    def weight_part(member, half):
        place = (own ^ member) * (2 * side) + half * side
        return lax.dynamic_slice(out_weight, (0, place), (out_weight.shape[0], side))

    def attend(head, blocks):
        return attention(head, core[None], starts, lambda_head, gain, queries, keys, values, blocks)

    slices = [weight_part(d, core) for d in (1, 2, 3)]
    two = later(here, 2)
    four = later(after(here, *slices), 4)
    mine = [weight_partner(part, d) for part, d in zip(slices, (1, 2, 3))]
    other = across(jnp.where(core == 0, here, four))
    blocks = [across(two), two, other, four]
    first = attend(0, blocks)
    gathered = [partner(first, d) for d in (1, 2, 3)]
    second = attend(1, blocks)
    far = jnp.concatenate(mine, axis=0)
    swapped = across(after(far, first))
    second, gathered[0] = after((second, gathered[0]), second)
    both = [first, *gathered, second] + [partner(second, d) for d in (1, 2, 3)]
    partial = project(both, [weight_part(0, core), far, weight_part(0, 1 - core), swapped])
    count = lax.axis_size("tp")
    parts = lax.all_to_all(partial.reshape(count, TOK // count, 2 * side), "tp", 0, 0)
    return total_up(core[None], parts)


def solution(mesh):
    return jax.shard_map(
        shards,
        mesh=mesh,
        in_specs=(
            P("ctx", "tp"),
            P("ctx", "tp"),
            P("ctx", "tp"),
            P("ctx"),
            P("tp", None),
            P("tp", None),
            P(),
            P("tp", None),
        ),
        out_specs=P(("ctx", "tp"), None),
        check_vma=False,
    )
```
